32 devices in a mesh: parts: 2 (over x), leaf: 16 (over z, y, core).
Axes of the slice: x: 2, y: 2, z: 4, core: 2. Of those that a mesh axis runs over, the one named last changes fastest.
Arguments:
- rhs: bfloat16 [131072, 384], P(('parts', 'leaf')), parts along dimension 0, may hold values from -6 to 6
- left_basis: bfloat16 [2, 131072, 64], P(None, ('parts', 'leaf')), parts along dimension 1, may hold values from -0.0625 to 0.0625
- right_basis: bfloat16 [2, 131072, 64], P(None, ('parts', 'leaf')), parts along dimension 1, may hold values from -0.5 to 0.5
- near_field: bfloat16 [2, 512, 256, 256], P(None, ('parts', 'leaf')), parts along dimension 1, may hold values from -0.25 to 0.25
- factors: bfloat16 [32, 4, 2, 2, 64, 64], P(('parts', 'leaf')), parts along dimension 0, may hold values from -0.375 to 0.375
- coupling: bfloat16 [32, 16, 2, 64, 64], P(('parts', 'leaf')), parts along dimension 0, may hold values from -0.125 to 0.125
- pattern: int32 [32, 4, 4], P(('parts', 'leaf')), parts along dimension 0, may hold values 0 or 1
- leaf_order: int32 [32, 16], P(('parts', 'leaf')), parts along dimension 0, may hold values from 0 to 15, each once within a row
Outputs:
- product: bfloat16 [131072, 384], P(('parts', 'leaf')), parts along dimension 0
The draws below stay inside these ranges and needn't reach their ends.
There are 2 independent parts, one for each index of `parts`. The reference program is written for one: setup_inputs(seed, part) draws one part's arguments, and reference() takes and returns one part's arrays. A program takes and returns all parts, laid end to end along the dimension named above; each array names one. Nothing has to cross between parts.
Inputs may be any that keep to these rules, and one draw needn't show every extreme that they name: `leaf_order`: each row names every slot of the group exactly once.
All inputs are finite; a program needn't handle non-finite values. No bound on the sum of `pattern` on one device may be relied on, other than what follows from the above.
Results may differ from the reference program's by a relative error of at most 0.0065.
Values may be sent and summed in bfloat16 or wider, within the bound.
No kernel may reach another device: no remote copies, remote signals or barrier semaphores. Data moves between devices by JAX's collectives and lax.ppermute only.
A program may use at most 128 MiB of HBM per device.

```python
import jax
import jax.numpy as jnp
from jax import lax

K = 64
NRHS = 192
COLS = 384
PTS = 4096
LB = 256
NB = 4
GROUP = 16
LEVELS = 4
NBOX = 16
NPTS = 65536
NBOXES = 256
N_LEAF = 16


def touch_ends(values, stream_key, least, top_value):
    extent = values.shape
    index_at = [jax.random.randint(jax.random.fold_in(stream_key, axis), (), 0, extent[axis]) for axis in range(len(extent))]
    values = values.at[tuple(index_at)].set(least)
    longest = extent.index(max(extent))
    index_at[longest] = (index_at[longest] + 1) % extent[longest]
    return values.at[tuple(index_at)].set(top_value)


def shard_levels(stream_key, extent, split, least, high):
    def one(dim, shards_of):
        heights = jax.random.uniform(jax.random.fold_in(jax.random.fold_in(stream_key, 6), dim), (shards_of,), jnp.float32, least / len(split), high / len(split))
        return jnp.repeat(jnp.exp(heights), extent[dim] // shards_of).reshape((-1,) + (1,) * (len(extent) - dim - 1))

    factor_of = one(*split[0])
    for cut in split[1:]:
        factor_of = factor_of * one(*cut)
    return factor_of


def noise(rng, shape, width, reach, shards=(), kind=jnp.bfloat16):
    loudness = shard_levels(rng, shape, shards, -0.22, 0.18) if shards else 1.0
    values = jax.random.normal(rng, shape, jnp.float32) * width * loudness
    return jnp.minimum(jnp.maximum(values, -reach), reach).astype(kind)


def setup_inputs(seed: int = 0, part: int = 0) -> dict:
    keys = jax.random.split(jax.random.key(seed), 9)
    part_keys = jax.random.split(jax.random.fold_in(keys[8], part), 9)
    return {
        "rhs": noise(part_keys[0], (NPTS, COLS), 1.0, 6.0, ((0, 16),)),
        "left_basis": noise(part_keys[1], (2, NPTS, K), (2 * PTS) ** -0.5, 0.0625, ((1, 16),)),
        "right_basis": noise(part_keys[2], (2, NPTS, K), (2 * K) ** -0.5, 0.5, ((1, 16),)),
        "near_field": noise(part_keys[3], (2, NBOXES, LB, LB), (2 * LB) ** -0.5, 0.25, ((1, 16),)),
        "factors": noise(part_keys[4], (N_LEAF, LEVELS, 2, 2, K, K), (4 * K) ** -0.5, 0.375, ((0, 16),)),
        "coupling": noise(part_keys[5], (N_LEAF, GROUP, 2, K, K), (2 * GROUP * K) ** -0.5, 0.125, ((0, 16),)),
        "pattern": touch_ends((jax.random.randint(part_keys[6], (N_LEAF, LEVELS, NB), 0, 4) < 3).astype(jnp.int32), jax.random.fold_in(part_keys[6], 1), 0, 1),
        "leaf_order": jax.vmap(lambda own: jax.random.permutation(own, GROUP))(jax.random.split(part_keys[7], N_LEAF)).reshape((N_LEAF, GROUP)).astype(jnp.int32),
    }


def combine(prod_re, prod_im, half_cols):
    real_part = prod_re[..., :half_cols] - prod_im[..., half_cols:]
    imag_part = prod_re[..., half_cols:] + prod_im[..., :half_cols]
    return jnp.concatenate([real_part, imag_part], axis=-1)


def batch_apply(matrix, vectors, half_cols):
    matf = matrix.astype(jnp.float32)
    vecf = vectors.astype(jnp.float32)
    part_re = jnp.einsum('dik,dkc->dic', matf[:, 0], vecf)
    part_im = jnp.einsum('dik,dkc->dic', matf[:, 1], vecf)
    return combine(part_re, part_im, half_cols)


def reference(rhs, left_basis, right_basis, near_field, factors, coupling, pattern, leaf_order):
    half_cols = NRHS
    bit_count = N_LEAF.bit_length() - 1
    rhs_leaves = rhs.reshape(N_LEAF, PTS, COLS)
    left_split = left_basis.reshape(2, N_LEAF, PTS, K)
    right_split = right_basis.reshape(2, N_LEAF, PTS, K)
    near_split = near_field.reshape(2, N_LEAF, NBOX, LB, LB)

    def leaf_skeleton(packed):
        leaf_rhs, basis_re, basis_im = packed
        dims = (((0,), (0,)), ((), ()))
        part_re = lax.dot_general(basis_re, leaf_rhs, dims, preferred_element_type=jnp.float32)
        part_im = lax.dot_general(basis_im, leaf_rhs, dims, preferred_element_type=jnp.float32)
        return combine(part_re, part_im, half_cols).astype(jnp.bfloat16)

    skeleton = lax.map(leaf_skeleton, (rhs_leaves, left_split[0], left_split[1]))
    leaves = jnp.arange(N_LEAF, dtype=jnp.int32)
    for level_idx in range(LEVELS):
        bit_idx = bit_count - 1 - level_idx
        partner = skeleton[jnp.bitwise_xor(leaves, jnp.int32(1 << bit_idx))]
        row_mask = jnp.repeat(pattern[:, level_idx, :], K // NB, axis=1).astype(jnp.bfloat16)
        self_factor = factors[:, level_idx, 0]
        cross_factor = factors[:, level_idx, 1] * row_mask[:, None, :, None]
        mixed_sum = batch_apply(self_factor, skeleton, half_cols) + batch_apply(cross_factor, partner, half_cols)
        skeleton = mixed_sum.astype(jnp.bfloat16)

    member_idx = ((leaves // GROUP) * GROUP)[:, None] + leaf_order
    gathered = skeleton[member_idx].astype(jnp.float32)
    couple = coupling.astype(jnp.float32)
    part_re = jnp.einsum('djik,djkc->dic', couple[:, :, 0], gathered)
    part_im = jnp.einsum('djik,djkc->dic', couple[:, :, 1], gathered)
    coarse = combine(part_re, part_im, half_cols).astype(jnp.bfloat16)

    def leaf_output(packed):
        leaf_rhs, basis_re, basis_im, near_re, near_im, coarse_leaf = packed
        far_field = combine(jnp.dot(basis_re, coarse_leaf, preferred_element_type=jnp.float32),
                            jnp.dot(basis_im, coarse_leaf, preferred_element_type=jnp.float32), half_cols)
        rhs_boxes = leaf_rhs.reshape(NBOX, LB, COLS).astype(jnp.float32)
        near_term = combine(jnp.einsum('bij,bjc->bic', near_re.astype(jnp.float32), rhs_boxes),
                            jnp.einsum('bij,bjc->bic', near_im.astype(jnp.float32), rhs_boxes), half_cols)
        return (far_field + near_term.reshape(PTS, COLS)).astype(jnp.bfloat16)

    result = lax.map(leaf_output, (rhs_leaves, right_split[0], right_split[1], near_split[0], near_split[1], coarse))
    return result.reshape(NPTS, COLS)
```

```python
import functools

import jax
import jax.numpy as jnp
from jax import lax
from jax.experimental import pallas as pl
from jax.experimental.pallas import tpu as pltpu
from jax.sharding import PartitionSpec as P

BF = jnp.bfloat16
F32 = jnp.float32
VMEM = pl.BlockSpec(memory_space=pltpu.VMEM)
SMEM = pl.BlockSpec(memory_space=pltpu.SMEM)
ANY = pl.BlockSpec(memory_space=pl.ANY)
HBM = pl.BlockSpec(memory_space=pltpu.HBM)


def partner(array, apart):
    count = lax.axis_size("leaf")
    return lax.ppermute(array, "leaf", [(i, i ^ apart) for i in range(count)])


def in_hbm(array):
    return pltpu.with_memory_space_constraint(array, pltpu.HBM)


def turned(block):
    half = block.shape[1] // 2
    return jnp.concatenate([-block[:, half:], block[:, :half]], axis=1)


def combined(stacked):
    rank = stacked.shape[0] // 2
    return stacked[:rank] + turned(stacked[rank:])


def dot(a, b):
    return jnp.dot(a, b, preferred_element_type=F32)


def params(mib):
    return pltpu.CompilerParams(vmem_limit_bytes=mib * 2**20)


def cost(flops, moved):
    return pl.CostEstimate(flops=flops, bytes_accessed=moved, transcendentals=0)


def project_kernel(chunks, left, rhs, factors, pattern, skel, rhs_keep, mixers, left_buf, fac_buf, sems):
    depth = rhs.shape[0] // chunks
    rank = left.shape[1]
    fac_copy = pltpu.make_async_copy(factors, fac_buf, sems.at[2 * chunks])
    copies = []
    for c in range(chunks):
        span = pl.ds(c * depth, depth)
        copies.append((
            pltpu.make_async_copy(left.at[:, :, span], left_buf.at[:, :, span], sems.at[2 * c]),
            pltpu.make_async_copy(rhs.at[span], rhs_keep.at[span], sems.at[2 * c + 1]),
        ))
    for one, two in copies[:1]:
        one.start()
        two.start()
    fac_copy.start()
    for one, two in copies[1:]:
        one.start()
        two.start()
    fac_copy.wait()
    levels = factors.shape[0]
    blocks = pattern.shape[1]
    row_block = lax.broadcasted_iota(jnp.int32, (rank, rank), 0) // (rank // blocks)
    for level in range(levels):
        keep = jnp.zeros((rank, rank), F32)
        for r in range(blocks):
            keep = jnp.where(row_block == r, pattern[level, r].astype(F32), keep)
        for part in range(2):
            own = fac_buf[level, 0, part]
            cross = (fac_buf[level, 1, part].astype(F32) * keep).astype(BF)
            mixers[level, pl.ds(part * rank, rank), :] = jnp.concatenate([own, cross], axis=1)
    total = jnp.zeros((2 * rank, rhs.shape[1]), F32)
    for c in range(chunks):
        span = pl.ds(c * depth, depth)
        copies[c][0].wait()
        copies[c][1].wait()
        total += dot(left_buf[:, :, span].reshape(2 * rank, depth), rhs_keep[span, :])
    skel[...] = combined(total).astype(BF)


def project(left_t, rhs, factors, pattern):
    chunks = 8
    rank = left_t.shape[1]
    levels = factors.shape[0]
    return pl.pallas_call(
        functools.partial(project_kernel, chunks),
        out_shape=(
            pltpu.VMEM((rank, rhs.shape[1]), BF),
            pltpu.VMEM(rhs.shape, BF),
            pltpu.VMEM((levels, 2 * rank, 2 * rank), BF),
        ),
        in_specs=[HBM, HBM, HBM, SMEM],
        out_specs=(VMEM, VMEM, VMEM),
        scratch_shapes=[
            pltpu.VMEM(left_t.shape, BF),
            pltpu.VMEM(factors.shape, BF),
            pltpu.SemaphoreType.DMA((2 * chunks + 1,)),
        ],
        compiler_params=params(8),
        cost_estimate=cost(4 * left_t.size * rhs.shape[1], 2 * (left_t.size + rhs.size)),
        name="project",
    )(left_t, rhs, factors, pattern)


def near_kernel(first, near, rhs_keep, out, token, buf, sems):
    count = buf.shape[1]
    width = buf.shape[2]
    copies = []
    for b in range(count):
        copies.append(pltpu.make_async_copy(near.at[:, first + b], buf.at[:, b], sems.at[b]))
        copies[-1].start()
    for b in range(count):
        block = rhs_keep[pl.ds((first + b) * width, width), :]
        side = turned(block)
        copies[b].wait()
        out[pl.ds(b * width, width), :] = dot(buf[0, b], block) + dot(buf[1, b], side)
    token[...] = jnp.zeros_like(token)


def near_part(near, rhs_keep, first, count):
    width = near.shape[2]
    cols = rhs_keep.shape[1]
    return pl.pallas_call(
        functools.partial(near_kernel, first),
        out_shape=(pltpu.VMEM((count * width, cols), F32), jax.ShapeDtypeStruct((8, 128), F32)),
        in_specs=[HBM, VMEM],
        out_specs=(VMEM, VMEM),
        scratch_shapes=[
            pltpu.VMEM((2, count, width, width), BF),
            pltpu.SemaphoreType.DMA((count,)),
        ],
        compiler_params=params(8),
        cost_estimate=cost(4 * count * width * width * cols, 4 * count * width * width),
        name="near_part",
    )(near, rhs_keep)


def prepare_kernel(chunks, members, right, coupling, order, here, token, right_rows, table, right_buf, couple_buf, slot, sems):
    rank = right.shape[1]
    rows = right.shape[2]
    depth = rows // chunks
    group = coupling.shape[0]
    first = pltpu.make_async_copy(coupling, couple_buf, sems.at[0])
    second = pltpu.make_async_copy(right, right_buf, sems.at[1])
    first.start()
    second.start()
    for j in range(group):
        slot[order[0, j] ^ here[0]] = j
    first.wait()
    per = len(members[0])
    for row in range(len(members)):
        for part in range(2):
            pieces = [couple_buf[slot[members[row][i]], part] for i in range(per)]
            table[row, pl.ds(part * rank, rank), :] = jnp.concatenate(pieces, axis=1)
    second.wait()
    for c in range(chunks):
        span = pl.ds(c * depth, depth)
        right_rows[span, :] = right_buf[:, :, span].reshape(2 * rank, depth).T


def prepare(right_t, coupling, order, here, members, token):
    chunks = 8
    rank = right_t.shape[1]
    rows = right_t.shape[2]
    return pl.pallas_call(
        functools.partial(prepare_kernel, chunks, members),
        out_shape=(
            pltpu.VMEM((rows, 2 * rank), BF),
            pltpu.VMEM((len(members), 2 * rank, len(members[0]) * rank), BF),
        ),
        in_specs=[HBM, HBM, SMEM, SMEM, ANY],
        out_specs=(VMEM, VMEM),
        scratch_shapes=[
            pltpu.VMEM(right_t.shape, BF),
            pltpu.VMEM(coupling.shape, BF),
            pltpu.SMEM((coupling.shape[0],), jnp.int32),
            pltpu.SemaphoreType.DMA((2,)),
        ],
        compiler_params=params(8),
        cost_estimate=cost(right_t.size, 4 * right_t.size + 4 * coupling.size),
        name="prepare",
    )(right_t, coupling, order, here, token)


def level_kernel(level, mixers, skel, other, token, out):
    both = jnp.concatenate([skel[...], other[...]], axis=0)
    out[...] = combined(dot(mixers[level], both)).astype(BF)


def level_step(level, mixers, skel, other, token):
    return pl.pallas_call(
        functools.partial(level_kernel, level),
        out_shape=pltpu.VMEM(skel.shape, BF),
        in_specs=[VMEM, VMEM, VMEM, ANY],
        out_specs=VMEM,
        cost_estimate=cost(8 * skel.shape[0] * skel.size, 6 * skel.size),
        name="level_step",
    )(mixers, skel, other, token)


def fork_step(level, mixers, level_other, mixers_other, skel, other, token):
    rank, cols = skel.shape

    def kernel(mix, mix_other, own, far, token, out):
        a = own[...]
        b = far[...]
        out[:rank, :] = combined(dot(mix[level], jnp.concatenate([a, b], axis=0))).astype(BF)
        out[rank:, :] = combined(dot(mix_other[level_other], jnp.concatenate([b, a], axis=0))).astype(BF)

    return pl.pallas_call(
        kernel,
        out_shape=pltpu.VMEM((2 * rank, cols), BF),
        in_specs=[VMEM, VMEM, VMEM, VMEM, ANY],
        out_specs=VMEM,
        cost_estimate=cost(16 * rank * skel.size, 8 * skel.size),
        name="fork_step",
    )(mixers, mixers_other, skel, other, token)


def twin_step(level, mixers, level_other, mixers_other, pair, other):
    rank = pair.shape[0] // 2

    def kernel(mix, mix_other, own, far, out):
        a = own[...]
        b = far[...]
        out[:rank, :] = combined(dot(mix[level], jnp.concatenate([a[:rank], b[:rank]], axis=0))).astype(BF)
        out[rank:, :] = combined(dot(mix_other[level_other], jnp.concatenate([a[rank:], b[rank:]], axis=0))).astype(BF)

    return pl.pallas_call(
        kernel,
        out_shape=pltpu.VMEM(pair.shape, BF),
        in_specs=[VMEM, VMEM, VMEM, VMEM],
        out_specs=VMEM,
        cost_estimate=cost(16 * rank * pair.size, 8 * pair.size),
        name="twin_step",
    )(mixers, mixers_other, pair, other)


def finish_kernel(n_blocks, n_near, chunks, *refs):
    blocks = refs[:n_blocks]
    nears = refs[n_blocks:n_blocks + n_near]
    table, right_rows, out, buf, sems = refs[n_blocks + n_near:]
    per = table.shape[2] // blocks[0].shape[0]
    total = None
    for row in range(table.shape[0]):
        stack = [ref[...] for ref in blocks[row * per:(row + 1) * per]]
        both = stack[0] if per == 1 else jnp.concatenate(stack, axis=0)
        term = dot(table[row], both)
        total = term if total is None else total + term
    coarse = combined(total).astype(BF)
    weights = jnp.concatenate([coarse, turned(coarse)], axis=0)
    rows = buf.shape[0]
    depth = rows // chunks
    span_near = rows // n_near
    copies = []
    for c in range(chunks):
        span = pl.ds(c * depth, depth)
        which, at = divmod(c * depth, span_near)
        value = dot(right_rows[span, :], weights) + nears[which][pl.ds(at, depth), :]
        buf[span, :] = value.astype(BF)
        copies.append(pltpu.make_async_copy(buf.at[span], out.at[span], sems.at[c]))
        copies[-1].start()
    for copy in copies:
        copy.wait()


def finish(blocks, nears, table, right_rows):
    chunks = 8
    rows = right_rows.shape[0]
    cols = blocks[0].shape[1]
    return pl.pallas_call(
        functools.partial(finish_kernel, len(blocks), len(nears), chunks),
        out_shape=jax.ShapeDtypeStruct((rows, cols), BF),
        in_specs=[VMEM] * (len(blocks) + len(nears) + 2),
        out_specs=ANY,
        scratch_shapes=[pltpu.VMEM((rows, cols), BF), pltpu.SemaphoreType.DMA((chunks,))],
        compiler_params=params(8),
        cost_estimate=cost(2 * rows * right_rows.shape[1] * cols, 6 * rows * cols),
        name="finish",
    )(*blocks, *nears, table, right_rows)


def per_device(rhs, left_basis, right_basis, near_field, factors, coupling, pattern, leaf_order):
    leaves = lax.axis_size("leaf")
    bits = leaves.bit_length() - 1
    levels = factors.shape[1]
    group = leaf_order.shape[1]
    boxes = near_field.shape[1]
    left_t = in_hbm(jnp.swapaxes(left_basis, 1, 2))
    right_t = in_hbm(jnp.swapaxes(right_basis, 1, 2))
    near_field = in_hbm(near_field)
    couple = in_hbm(coupling[0])
    here = (lax.axis_index("leaf") % group).astype(jnp.int32)[None]

    skel, rhs_keep, mixers = project(left_t, in_hbm(rhs), in_hbm(factors[0]), pattern[0])
    parts = 4
    nears = []

    def near_next():
        value, token = near_part(near_field, rhs_keep, len(nears) * (boxes // parts), boxes // parts)
        nears.append(value)
        return token

    if leaves == group == 16 and levels == 4:
        mixers_other = partner(mixers[2:], 2)
        skel = level_step(0, mixers, skel, partner(skel, 8), near_next())
        skel = level_step(1, mixers, skel, partner(skel, 4), near_next())
        pair = fork_step(2, mixers, 0, mixers_other, skel, partner(skel, 2), near_next())
        pair = twin_step(3, mixers, 1, mixers_other, pair, partner(pair, 1))
        zs = [pair] + [partner(pair, 4 * k) for k in (3, 2, 1)]
        token = near_next()
        members = tuple((4 * k, 4 * k + 2, 4 * k + 1, 4 * k + 3) for k in (0, 3, 2, 1))
        right_rows, table = prepare(right_t, couple, leaf_order, here, members, token)
        *far, right_rows, table = lax.optimization_barrier((*zs[1:], right_rows, table))
        zs = [pair] + far
        blocks = []
        for block in zs:
            blocks += [block, partner(block, 1)]
    else:
        for level in range(levels):
            token = near_next() if len(nears) < parts else jnp.zeros((8, 128), F32)
            skel = level_step(level, mixers, skel, partner(skel, 1 << (bits - 1 - level)), token)
        while len(nears) < parts:
            token = near_next()
        blocks = [skel]
        for bit in reversed(range(group.bit_length() - 1)):
            stack = jnp.stack(blocks)
            other = partner(stack, 1 << bit)
            blocks = blocks + [other[i] for i in range(len(blocks))]
        names = [0]
        for bit in reversed(range(group.bit_length() - 1)):
            names = names + [n ^ (1 << bit) for n in names]
        members = tuple(tuple(names[i:i + 4]) for i in range(0, group, 4))
        right_rows, table = prepare(right_t, couple, leaf_order, here, members, token)
    return finish(blocks, nears, table, right_rows)


def solution(mesh):
    both = ("parts", "leaf")
    in_specs = (
        P(both, None),
        P(None, both, None),
        P(None, both, None),
        P(None, both, None, None),
        P(both, None, None, None, None, None),
        P(both, None, None, None, None),
        P(both, None, None),
        P(both, None),
    )
    return jax.shard_map(
        per_device, mesh=mesh, in_specs=in_specs, out_specs=P(both, None), check_vma=False
    )
```

```python
import functools

import jax
import jax.numpy as jnp
from jax import lax
from jax.experimental import pallas as pl
from jax.experimental.pallas import tpu as pltpu
from jax.sharding import PartitionSpec as P

BF = jnp.bfloat16
F32 = jnp.float32
VMEM = pl.BlockSpec(memory_space=pltpu.VMEM)
SMEM = pl.BlockSpec(memory_space=pltpu.SMEM)
ANY = pl.BlockSpec(memory_space=pl.ANY)
HBM = pl.BlockSpec(memory_space=pltpu.HBM)


def partner(array, apart):
    count = lax.axis_size("leaf")
    return lax.ppermute(array, "leaf", [(i, i ^ apart) for i in range(count)])


def in_hbm(array):
    return pltpu.with_memory_space_constraint(array, pltpu.HBM)


def turned(block):
    half = block.shape[1] // 2
    return jnp.concatenate([-block[:, half:], block[:, :half]], axis=1)


def combined(stacked):
    rank = stacked.shape[0] // 2
    return stacked[:rank] + turned(stacked[rank:])


def dot(a, b):
    return jnp.dot(a, b, preferred_element_type=F32)


def params(mib):
    return pltpu.CompilerParams(vmem_limit_bytes=mib * 2**20)


def cost(flops, moved):
    return pl.CostEstimate(flops=flops, bytes_accessed=moved, transcendentals=0)


def project_kernel(cuts, left, rhs, skel, rhs_keep, left_buf, sems):
    rank = left.shape[1]
    copies = []
    start = 0
    for c, depth in enumerate(cuts):
        span = pl.ds(start, depth)
        copies.append((
            span,
            pltpu.make_async_copy(left.at[:, :, span], left_buf.at[:, :, span], sems.at[2 * c]),
            pltpu.make_async_copy(rhs.at[span], rhs_keep.at[span], sems.at[2 * c + 1]),
        ))
        start += depth
    for _, one, two in copies:
        one.start()
        two.start()
    total = None
    for span, one, two in copies:
        one.wait()
        two.wait()
        term = dot(left_buf[:, :, span].reshape(2 * rank, span.size), rhs_keep[span, :])
        total = term if total is None else total + term
    skel[...] = combined(total).astype(BF)


def project(left_t, rhs):
    rank = left_t.shape[1]
    rows = rhs.shape[0]
    cuts = (rows // 2, rows // 4, rows // 4)
    return pl.pallas_call(
        functools.partial(project_kernel, cuts),
        out_shape=(pltpu.VMEM((rank, rhs.shape[1]), BF), pltpu.VMEM(rhs.shape, BF)),
        in_specs=[HBM, HBM],
        out_specs=(VMEM, VMEM),
        scratch_shapes=[pltpu.VMEM(left_t.shape, BF), pltpu.SemaphoreType.DMA((2 * len(cuts),))],
        compiler_params=params(4),
        cost_estimate=cost(4 * left_t.size * rhs.shape[1], 2 * (left_t.size + rhs.size)),
        name="project",
    )(left_t, rhs)


def mixers_kernel(factors, pattern, after, first, rest, fac_buf, pat_buf, sems):
    levels = factors.shape[0]
    blocks = pattern.shape[1]
    rank = factors.shape[3]
    one = pltpu.make_async_copy(factors, fac_buf, sems.at[0])
    two = pltpu.make_async_copy(pattern, pat_buf, sems.at[1])
    one.start()
    two.start()
    one.wait()
    two.wait()
    high = rank // blocks
    for level in range(levels):
        out, at = (first, 0) if level == 0 else (rest, level - 1)
        for part in range(2):
            own = fac_buf[level, 0, part]
            cross = fac_buf[level, 1, part].astype(F32)
            pieces = [cross[r * high:(r + 1) * high, :] * pat_buf[level, r].astype(F32) for r in range(blocks)]
            masked = jnp.concatenate(pieces, axis=0).astype(BF)
            out[at, pl.ds(part * rank, rank), :] = jnp.concatenate([own, masked], axis=1)


def make_mixers(factors, pattern, after):
    levels = factors.shape[0]
    rank = factors.shape[3]
    return pl.pallas_call(
        mixers_kernel,
        out_shape=(
            pltpu.VMEM((1, 2 * rank, 2 * rank), BF),
            pltpu.VMEM((levels - 1, 2 * rank, 2 * rank), BF),
        ),
        in_specs=[HBM, HBM, ANY],
        out_specs=(VMEM, VMEM),
        scratch_shapes=[
            pltpu.VMEM(factors.shape, BF),
            pltpu.SMEM(pattern.shape, jnp.int32),
            pltpu.SemaphoreType.DMA((2,)),
        ],
        compiler_params=params(2),
        cost_estimate=cost(factors.size, 4 * factors.size),
        name="mixers",
    )(factors, pattern, after)


def behind_kernel(members, groups, near, rhs_keep, right, coupling, order, here, after,
                  out, right_rows, table, buf, right_buf, couple_buf, slot, sems):
    rank = right.shape[1]
    rows = right.shape[2]
    boxes, width = near.shape[1], near.shape[2]
    group = coupling.shape[0]
    each = boxes // groups
    copies = []
    for g in range(groups):
        span = pl.ds(g * each, each)
        copies.append(pltpu.make_async_copy(near.at[:, span], buf.at[:, span], sems.at[g]))
    couple_copy = pltpu.make_async_copy(coupling, couple_buf, sems.at[groups])
    right_copy = pltpu.make_async_copy(right, right_buf, sems.at[groups + 1])
    right_copy.start()
    couple_copy.start()
    for copy in copies:
        copy.start()
    for j in range(group):
        slot[order[0, j] ^ here[0]] = j
    right_copy.wait()
    depth = rows // 8
    for c in range(8):
        span = pl.ds(c * depth, depth)
        right_rows[span, :] = right_buf[:, :, span].reshape(2 * rank, depth).T
    couple_copy.wait()
    per = len(members[0])
    for row in range(len(members)):
        for part in range(2):
            pieces = [couple_buf[slot[members[row][i]], part] for i in range(per)]
            table[row, pl.ds(part * rank, rank), :] = jnp.concatenate(pieces, axis=1)
    for g in range(groups):
        copies[g].wait()
        for b in range(g * each, (g + 1) * each):
            rows_b = pl.ds(b * width, width)
            block = rhs_keep[rows_b, :]
            out[rows_b, :] = dot(buf[0, b], block) + dot(buf[1, b], turned(block))


def behind(near, rhs_keep, right_t, coupling, order, here, members, after):
    groups = 4
    rank = right_t.shape[1]
    rows = right_t.shape[2]
    width = near.shape[2]
    cols = rhs_keep.shape[1]
    return pl.pallas_call(
        functools.partial(behind_kernel, members, groups),
        out_shape=(
            pltpu.VMEM((rows, cols), F32),
            pltpu.VMEM((rows, 2 * rank), BF),
            pltpu.VMEM((len(members), 2 * rank, len(members[0]) * rank), BF),
        ),
        in_specs=[HBM, VMEM, HBM, HBM, SMEM, SMEM, ANY],
        out_specs=(VMEM, VMEM, VMEM),
        scratch_shapes=[
            pltpu.VMEM(near.shape, BF),
            pltpu.VMEM(right_t.shape, BF),
            pltpu.VMEM(coupling.shape, BF),
            pltpu.SMEM((coupling.shape[0],), jnp.int32),
            pltpu.SemaphoreType.DMA((groups + 2,)),
        ],
        compiler_params=params(10),
        cost_estimate=cost(4 * rows * width * cols, 2 * near.size + 2 * right_t.size + 4 * coupling.size),
        name="behind",
    )(near, rhs_keep, right_t, coupling, order, here, after)


def mixed(matrix, one, two):
    return combined(dot(matrix, jnp.concatenate([one, two], axis=0))).astype(BF)


def level_kernel(level, mixers, skel, other, out):
    out[...] = mixed(mixers[level], skel[...], other[...])


def level_step(level, mixers, skel, other):
    return pl.pallas_call(
        functools.partial(level_kernel, level),
        out_shape=pltpu.VMEM(skel.shape, BF),
        in_specs=[VMEM, VMEM, VMEM],
        out_specs=VMEM,
        compiler_params=params(1),
        cost_estimate=cost(8 * skel.shape[0] * skel.size, 6 * skel.size),
        name="level_step",
    )(mixers, skel, other)


def quad_kernel(mix, mix_y, skel, skel_z, skel_y, skel_zy, out):
    rank = skel.shape[0]
    here = mixed(mix[0], skel[...], skel_z[...])
    there = mixed(mix_y[0], skel_y[...], skel_zy[...])
    out[:rank, :] = mixed(mix[1], here, there)
    out[rank:, :] = mixed(mix_y[1], there, here)


def quad_step(mix, mix_y, skel, skel_z, skel_y, skel_zy):
    rank, cols = skel.shape
    return pl.pallas_call(
        quad_kernel,
        out_shape=pltpu.VMEM((2 * rank, cols), BF),
        in_specs=[VMEM] * 6,
        out_specs=VMEM,
        compiler_params=params(1),
        cost_estimate=cost(32 * rank * skel.size, 12 * skel.size),
        name="quad_step",
    )(mix, mix_y, skel, skel_z, skel_y, skel_zy)


def twin_kernel(mix, mix_y, pair, far, out):
    rank = pair.shape[0] // 2
    out[:rank, :] = mixed(mix[2], pair[:rank, :], far[:rank, :])
    out[rank:, :] = mixed(mix_y[2], pair[rank:, :], far[rank:, :])


def twin_step(mix, mix_y, pair, far):
    return pl.pallas_call(
        twin_kernel,
        out_shape=pltpu.VMEM(pair.shape, BF),
        in_specs=[VMEM] * 4,
        out_specs=VMEM,
        compiler_params=params(1),
        cost_estimate=cost(8 * pair.shape[0] * pair.size, 8 * pair.size),
        name="twin_step",
    )(mix, mix_y, pair, far)


def finish_kernel(n_blocks, chunks, *refs):
    blocks = refs[:n_blocks]
    near, table, right_rows, out, buf, sems = refs[n_blocks:]
    per = table.shape[2] // blocks[0].shape[0]
    total = None
    for row in range(table.shape[0]):
        both = jnp.concatenate([ref[...] for ref in blocks[row * per:(row + 1) * per]], axis=0)
        term = dot(table[row], both)
        total = term if total is None else total + term
    coarse = combined(total).astype(BF)
    weights = jnp.concatenate([coarse, turned(coarse)], axis=0)
    depth = buf.shape[0] // chunks
    copies = []
    for c in range(chunks):
        span = pl.ds(c * depth, depth)
        buf[span, :] = (dot(right_rows[span, :], weights) + near[span, :]).astype(BF)
        copies.append(pltpu.make_async_copy(buf.at[span], out.at[span], sems.at[c]))
        copies[-1].start()
    for copy in copies:
        copy.wait()


def finish(blocks, near, table, right_rows):
    chunks = 8
    rows, cols = near.shape
    return pl.pallas_call(
        functools.partial(finish_kernel, len(blocks), chunks),
        out_shape=jax.ShapeDtypeStruct((rows, cols), BF),
        in_specs=[VMEM] * (len(blocks) + 3),
        out_specs=ANY,
        scratch_shapes=[pltpu.VMEM((rows, cols), BF), pltpu.SemaphoreType.DMA((chunks,))],
        compiler_params=params(8),
        cost_estimate=cost(2 * rows * right_rows.shape[1] * cols, 6 * rows * cols),
        name="finish",
    )(*blocks, near, table, right_rows)


def per_device(rhs, left_basis, right_basis, near_field, factors, coupling, pattern, leaf_order):
    leaves = lax.axis_size("leaf")
    bits = leaves.bit_length() - 1
    levels = factors.shape[1]
    group = leaf_order.shape[1]
    boxes = near_field.shape[1]
    left_t = in_hbm(jnp.swapaxes(left_basis, 1, 2))
    right_t = in_hbm(jnp.swapaxes(right_basis, 1, 2))
    near_field = in_hbm(near_field)
    couple = in_hbm(coupling[0])
    here = (lax.axis_index("leaf") % group).astype(jnp.int32)[None]

    skel, rhs_keep = project(left_t, in_hbm(rhs))
    first, rest = make_mixers(in_hbm(factors[0]), in_hbm(pattern[0]), skel)
    run_behind = functools.partial(behind, near_field, rhs_keep, right_t, couple, leaf_order, here)

    if leaves == group == 16 and levels == 4:
        rest_y = partner(rest, 2)
        skel = level_step(0, first, skel, partner(skel, 8))
        pair = quad_step(rest, rest_y, skel, partner(skel, 4), partner(skel, 2), partner(skel, 6))
        pair = twin_step(rest, rest_y, pair, partner(pair, 1))
        far = [partner(pair, 4 * k) for k in (3, 2, 1)]
        members = tuple((4 * k, 4 * k + 2, 4 * k + 1, 4 * k + 3) for k in (0, 3, 2, 1))
        near, right_rows, table = run_behind(members, pair)
        blocks = [pair, partner(pair, 1)]
        for block in far:
            block, table = lax.optimization_barrier((block, table))
            blocks += [block, partner(block, 1)]
    else:
        for level in range(levels):
            matrix, at = (first, 0) if level == 0 else (rest, level - 1)
            skel = level_step(at, matrix, skel, partner(skel, 1 << (bits - 1 - level)))
        blocks = [skel]
        names = [0]
        for bit in reversed(range(group.bit_length() - 1)):
            other = partner(jnp.stack(blocks), 1 << bit)
            blocks = blocks + [other[i] for i in range(len(blocks))]
            names = names + [n ^ (1 << bit) for n in names]
        members = tuple(tuple(names[i:i + 4]) for i in range(0, group, 4))
        near, right_rows, table = run_behind(members, skel)
    return finish(blocks, near, table, right_rows)


def solution(mesh):
    both = ("parts", "leaf")
    in_specs = (
        P(both, None),
        P(None, both, None),
        P(None, both, None),
        P(None, both, None, None),
        P(both, None, None, None, None, None),
        P(both, None, None, None, None),
        P(both, None, None),
        P(both, None),
    )
    return jax.shard_map(
        per_device, mesh=mesh, in_specs=in_specs, out_specs=P(both, None), check_vma=False
    )
```

```python
import functools

import jax
import jax.numpy as jnp
from jax import lax
from jax.experimental import pallas as pl
from jax.experimental.pallas import tpu as pltpu
from jax.sharding import PartitionSpec as P

BF = jnp.bfloat16
F32 = jnp.float32
VMEM = pl.BlockSpec(memory_space=pltpu.VMEM)
SMEM = pl.BlockSpec(memory_space=pltpu.SMEM)
ANY = pl.BlockSpec(memory_space=pl.ANY)
HBM = pl.BlockSpec(memory_space=pltpu.HBM)


def partner(array, apart):
    count = lax.axis_size("leaf")
    return lax.ppermute(array, "leaf", [(i, i ^ apart) for i in range(count)])


def in_hbm(array):
    return pltpu.with_memory_space_constraint(array, pltpu.HBM)


def turned(block):
    half = block.shape[1] // 2
    return jnp.concatenate([-block[:, half:], block[:, :half]], axis=1)


def combined(stacked):
    rank = stacked.shape[0] // 2
    return stacked[:rank] + turned(stacked[rank:])


def dot(a, b):
    return jnp.dot(a, b, preferred_element_type=F32)


def params(mib):
    return pltpu.CompilerParams(vmem_limit_bytes=mib * 2**20)


def cost(flops, moved):
    return pl.CostEstimate(flops=flops, bytes_accessed=moved, transcendentals=0)


def open_kernel(cuts, orders, left, rhs, factors, pattern, coupling, order, here, *refs):
    skel, rhs_keep, first, rest = refs[:4]
    tables = refs[4:4 + len(orders)]
    left_buf, fac_buf, pat_buf, couple_buf, order_buf, slot, sems = refs[4 + len(orders):]
    levels, blocks = pattern.shape
    rank = left.shape[1]
    high = rank // blocks
    ahead = (
        pltpu.make_async_copy(factors, fac_buf, sems.at[0]),
        pltpu.make_async_copy(pattern, pat_buf, sems.at[1]),
        pltpu.make_async_copy(order, order_buf, sems.at[2]),
        pltpu.make_async_copy(coupling, couple_buf, sems.at[3]),
    )
    copies = []
    start = 0
    for c, depth in enumerate(cuts):
        span = pl.ds(start, depth)
        copies.append((
            span,
            pltpu.make_async_copy(left.at[:, :, span], left_buf.at[:, :, span], sems.at[4 + 2 * c]),
            pltpu.make_async_copy(rhs.at[span], rhs_keep.at[span], sems.at[5 + 2 * c]),
        ))
        start += depth
    for copy in ahead:
        copy.start()
    for _, one, two in copies:
        one.start()
        two.start()
    ahead[0].wait()
    ahead[1].wait()
    for level in range(levels):
        out, at = (first, 0) if level == 0 else (rest, level - 1)
        for part in range(2):
            own = fac_buf[level, 0, part]
            cross = fac_buf[level, 1, part].astype(F32)
            pieces = [cross[r * high:(r + 1) * high, :] * pat_buf[level, r].astype(F32) for r in range(blocks)]
            masked = jnp.concatenate(pieces, axis=0).astype(BF)
            out[at, pl.ds(part * rank, rank), :] = jnp.concatenate([own, masked], axis=1)
    ahead[2].wait()
    for j in range(coupling.shape[0]):
        slot[order_buf[0, j] ^ here[0]] = j
    ahead[3].wait()
    for members, table in zip(orders, tables):
        for part in range(2):
            for i in range(0, len(members), 2):
                pair = [couple_buf[slot[m], part] for m in members[i:i + 2]]
                table[pl.ds(part * rank, rank), pl.ds(i * rank, 2 * rank)] = jnp.concatenate(pair, axis=1)
    total = None
    for span, one, two in copies:
        one.wait()
        two.wait()
        term = dot(left_buf[:, :, span].reshape(2 * rank, span.size), rhs_keep[span, :])
        total = term if total is None else total + term
    skel[...] = combined(total).astype(BF)


def open_step(left_t, rhs, factors, pattern, coupling, order, here, orders):
    rank = left_t.shape[1]
    rows = rhs.shape[0]
    cuts = (rows // 2, rows // 4, rows // 4)
    levels = factors.shape[0]
    outs = (
        pltpu.VMEM((rank, rhs.shape[1]), BF),
        pltpu.VMEM(rhs.shape, BF),
        pltpu.VMEM((1, 2 * rank, 2 * rank), BF),
        pltpu.VMEM((levels - 1, 2 * rank, 2 * rank), BF),
    ) + tuple(pltpu.VMEM((2 * rank, len(members) * rank), BF) for members in orders)
    return pl.pallas_call(
        functools.partial(open_kernel, cuts, orders),
        out_shape=outs,
        in_specs=[HBM] * 6 + [SMEM],
        out_specs=tuple(VMEM for _ in outs),
        scratch_shapes=[
            pltpu.VMEM(left_t.shape, BF),
            pltpu.VMEM(factors.shape, BF),
            pltpu.SMEM(pattern.shape, jnp.int32),
            pltpu.VMEM(coupling.shape, BF),
            pltpu.SMEM(order.shape, jnp.int32),
            pltpu.SMEM((coupling.shape[0],), jnp.int32),
            pltpu.SemaphoreType.DMA((4 + 2 * len(cuts),)),
        ],
        compiler_params=params(6),
        cost_estimate=cost(4 * left_t.size * rhs.shape[1], 2 * (left_t.size + rhs.size)),
        name="open_step",
    )(left_t, rhs, factors, pattern, coupling, order, here)


def near_kernel(groups, near, rhs, after, out, buf, sems):
    boxes, width = near.shape[1], near.shape[2]
    each = boxes // groups
    copies = []
    for g in range(groups):
        span = pl.ds(g * each, each)
        copies.append(pltpu.make_async_copy(near.at[:, span], buf.at[:, span], sems.at[g]))
        copies[-1].start()
    for g in range(groups):
        copies[g].wait()
        for b in range(g * each, (g + 1) * each):
            rows_b = pl.ds(b * width, width)
            block = rhs[rows_b, :]
            out[rows_b, :] = dot(buf[0, b], block) + dot(buf[1, b], turned(block))


def near_term(near, rhs, after):
    groups = 4
    rows, cols = rhs.shape
    return pl.pallas_call(
        functools.partial(near_kernel, groups),
        out_shape=pltpu.VMEM((rows, cols), F32),
        in_specs=[HBM, VMEM, ANY],
        out_specs=VMEM,
        scratch_shapes=[pltpu.VMEM(near.shape, BF), pltpu.SemaphoreType.DMA((groups,))],
        compiler_params=params(8),
        cost_estimate=cost(4 * rows * near.shape[2] * cols, 2 * near.size),
        name="near_term",
    )(near, rhs, after)


def mixed(matrix, one, two):
    return combined(dot(matrix, jnp.concatenate([one, two], axis=0))).astype(BF)


def level_kernel(level, mixers, skel, other, out):
    out[...] = mixed(mixers[level], skel[...], other[...])


def level_step(level, mixers, skel, other):
    return pl.pallas_call(
        functools.partial(level_kernel, level),
        out_shape=pltpu.VMEM(skel.shape, BF),
        in_specs=[VMEM, VMEM, VMEM],
        out_specs=VMEM,
        compiler_params=params(1),
        cost_estimate=cost(8 * skel.shape[0] * skel.size, 6 * skel.size),
        name="level_step",
    )(mixers, skel, other)


def quad_kernel(mix, mix_y, skel, skel_y, skel_zy, skel_z, out):
    rank = skel.shape[0]
    here = mixed(mix[0], skel[...], skel_z[...])
    there = mixed(mix_y[0], skel_y[...], skel_zy[...])
    out[:rank, :] = mixed(mix[1], here, there)
    out[rank:, :] = mixed(mix_y[1], there, here)


def quad_step(mix, mix_y, skel, skel_y, skel_zy, skel_z):
    rank, cols = skel.shape
    return pl.pallas_call(
        quad_kernel,
        out_shape=pltpu.VMEM((2 * rank, cols), BF),
        in_specs=[VMEM] * 6,
        out_specs=VMEM,
        compiler_params=params(1),
        cost_estimate=cost(32 * rank * skel.size, 12 * skel.size),
        name="quad_step",
    )(mix, mix_y, skel, skel_y, skel_zy, skel_z)


def twin_kernel(mix, mix_y, pair, far, out):
    rank = pair.shape[0] // 2
    out[:rank, :] = mixed(mix[2], pair[:rank, :], far[:rank, :])
    out[rank:, :] = mixed(mix_y[2], pair[rank:, :], far[rank:, :])


def twin_step(mix, mix_y, pair, far):
    return pl.pallas_call(
        twin_kernel,
        out_shape=pltpu.VMEM(pair.shape, BF),
        in_specs=[VMEM] * 4,
        out_specs=VMEM,
        compiler_params=params(1),
        cost_estimate=cost(8 * pair.shape[0] * pair.size, 8 * pair.size),
        name="twin_step",
    )(mix, mix_y, pair, far)


def couple_kernel(n_blocks, *refs):
    blocks, rest = refs[:n_blocks], refs[n_blocks:]
    half = len(rest) // 2
    stack = jnp.concatenate([ref[...] for ref in blocks], axis=0)
    for table, out in zip(rest[:half], rest[half:]):
        out[...] = combined(dot(table[...], stack))


def couple_step(blocks, tables):
    rank, cols = tables[0].shape[0] // 2, blocks[0].shape[1]
    outs = tuple(pltpu.VMEM((rank, cols), F32) for _ in tables)
    return pl.pallas_call(
        functools.partial(couple_kernel, len(blocks)),
        out_shape=outs,
        in_specs=[VMEM] * (len(blocks) + len(tables)),
        out_specs=tuple(VMEM for _ in outs),
        compiler_params=params(3),
        cost_estimate=cost(2 * len(tables) * tables[0].size * cols, 4 * rank * cols),
        name="couple_step",
    )(*blocks, *tables)


def finish_kernel(n_sums, chunks, *refs):
    sums = refs[:n_sums]
    near, right, out, buf, sems = refs[n_sums:]
    rank, rows = right.shape[1:]
    total = sums[0][...]
    for ref in sums[1:]:
        total += ref[...]
    coarse = total.astype(BF)
    weights = jnp.concatenate([coarse, turned(coarse)], axis=0)
    depth = rows // chunks
    copies = []
    for c in range(chunks):
        span = pl.ds(c * depth, depth)
        basis = right[:, :, span].reshape(2 * rank, depth)
        far = lax.dot_general(basis, weights, (((0,), (0,)), ((), ())), preferred_element_type=F32)
        buf[span, :] = (far + near[span, :]).astype(BF)
        copies.append(pltpu.make_async_copy(buf.at[span], out.at[span], sems.at[c]))
        copies[-1].start()
    for copy in copies:
        copy.wait()


def finish(sums, near, right_t):
    chunks = 8
    rows, cols = near.shape
    return pl.pallas_call(
        functools.partial(finish_kernel, len(sums), chunks),
        out_shape=jax.ShapeDtypeStruct((rows, cols), BF),
        in_specs=[VMEM] * (len(sums) + 2),
        out_specs=ANY,
        scratch_shapes=[pltpu.VMEM((rows, cols), BF), pltpu.SemaphoreType.DMA((chunks,))],
        compiler_params=params(6),
        cost_estimate=cost(2 * right_t.size * cols, 6 * rows * cols),
        name="finish",
    )(*sums, near, right_t)


def per_device(rhs, left_basis, right_basis, near_field, factors, coupling, pattern, leaf_order):
    leaves = lax.axis_size("leaf")
    bits = leaves.bit_length() - 1
    levels = factors.shape[1]
    group = leaf_order.shape[1]
    left_t = in_hbm(jnp.swapaxes(left_basis, 1, 2))
    right_t = jnp.swapaxes(right_basis, 1, 2)
    near_field = in_hbm(near_field)
    here = (lax.axis_index("leaf") & (group - 1)).astype(jnp.int32)[None]
    begin = functools.partial(open_step, left_t, in_hbm(rhs), in_hbm(factors[0]), in_hbm(pattern[0]), in_hbm(coupling[0]),
                              in_hbm(leaf_order), here)

    if leaves == group == 16 and levels == 4:
        far_order = (8, 4, 12)
        names = []
        for base in (0,) + far_order:
            names += [base, base ^ 2]
        skel, kept, first, rest, table, table_core = begin((tuple(names), tuple(n ^ 1 for n in names)))
        table_core = partner(table_core, 1)
        rest_y = partner(rest, 2)
        skel = level_step(0, first, skel, partner(skel, 8))
        side = {apart: partner(skel, apart) for apart in (4, 2, 6)}
        pair = quad_step(rest, rest_y, skel, side[2], side[6], side[4])
        pair = twin_step(rest, rest_y, pair, partner(pair, 1))
        far = [partner(pair, apart) for apart in far_order]
        near = near_term(near_field, kept, pair)
        *far, near = lax.optimization_barrier((*far, near))
        total_core, total = couple_step([pair] + far, [table_core, table])
        sums = [total, partner(total_core, 1)]
    else:
        names = (0,)
        for bit in reversed(range(group.bit_length() - 1)):
            names = names + tuple(n ^ (1 << bit) for n in names)
        skel, kept, first, rest, table = begin((names,))
        for level in range(levels):
            matrix, at = (first, 0) if level == 0 else (rest, level - 1)
            skel = level_step(at, matrix, skel, partner(skel, 1 << (bits - 1 - level)))
        blocks = [skel]
        for bit in reversed(range(group.bit_length() - 1)):
            other = partner(jnp.stack(blocks), 1 << bit)
            blocks = blocks + [other[i] for i in range(len(blocks))]
        near = near_term(near_field, kept, skel)
        sums = couple_step(blocks, [table])
    return finish(sums, near, right_t)


def solution(mesh):
    both = ("parts", "leaf")
    in_specs = (
        P(both, None),
        P(None, both, None),
        P(None, both, None),
        P(None, both, None, None),
        P(both, None, None, None, None, None),
        P(both, None, None, None, None),
        P(both, None, None),
        P(both, None),
    )
    return jax.shard_map(
        per_device, mesh=mesh, in_specs=in_specs, out_specs=P(both, None), check_vma=False
    )
```
